512 devices in a mesh: dp: 64 (over z, y), tensor: 8 (over x, core).
Axes of the slice: x: 4, y: 8, z: 8, core: 2. Of those that a mesh axis runs over, the one named last changes fastest.
Arguments:
- queries: bfloat16 [8192, 4, 8192], P('dp', None, 'tensor'), may hold values from -15 to 15
- grad_out: bfloat16 [8192, 4, 8192], P('dp', None, 'tensor'), may hold values from -6 to 6
- image_keys: bfloat16 [64, 768, 1024], P('dp', None, 'tensor'), may hold values from -4 to 4
- image_values: bfloat16 [64, 768, 1024], P('dp', None, 'tensor'), may hold values from -6 to 6
- gate_logits: float32 [64], P('tensor'), may hold values from -1.5 to 1.5
- tile_counts: int32 [64], P('dp'), may hold values from 1 to 3
- owners: int32 [8192, 1], P('dp'), may hold values from 0 to 63; in each aligned block of 128 rows (0 to 127, 128 to 255, ...) at most 3 rows name the same one
- text_only: int32 [8192], P('dp'), may hold values 0 or 1
Outputs:
- grad_queries: bfloat16 [8192, 4, 8192], P('dp', None, 'tensor')
- grad_keys: bfloat16 [64, 768, 1024], P('dp', None, 'tensor')
- grad_values: bfloat16 [64, 768, 1024], P('dp', None, 'tensor')
The draws below stay inside these ranges and needn't reach their ends.
Inputs may be any that keep to these rules, and one draw needn't show every extreme that they name: `owners`: of the rows of one device at most 3 name the same image, a bound that some block reaches of them.
All inputs are finite; a program needn't handle non-finite values. No bound on the sum of `text_only` on one device may be relied on, other than what follows from the above.
Results may differ from the reference program's by a relative error of at most 0.02.
Values may be sent and summed in bfloat16 or wider, within the bound.
No kernel may reach another device: no remote copies, remote signals or barrier semaphores. Data moves between devices by JAX's collectives and lax.ppermute only.
A program may use at most 64 MiB of HBM per device.

```python
import math
import jax
import jax.numpy as jnp
import numpy as np
from jax import lax

HEADS = 64
KV_HEADS = 8
HEAD = 128
TILE = 256
TILES_MAX = 3
SEG = 4
ROWS_DEV = 128
CAP = 3
ROWS = 8192
IMAGES = 64
KEYS = 768


def draw_queries(key, part):
    key = jax.random.fold_in(key, 3)
    first_key, second_key = jax.random.split(key)
    row_scale = jnp.exp(jax.random.uniform(second_key, (ROWS, SEG, 1), jnp.float32, math.log(0.3), math.log(3.0)))
    sample_base = jnp.clip(jax.random.normal(first_key, (ROWS, SEG, HEADS * HEAD), jnp.float32), -4.0, 4.0)
    result = sample_base * row_scale
    return result.astype(jnp.bfloat16)


def draw_image_keys(key, part):
    key = jax.random.fold_in(key, 5)
    result = jnp.clip(jax.random.normal(key, (IMAGES, KEYS, KV_HEADS * HEAD), jnp.float32), -4.0, 4.0)
    return result.astype(jnp.bfloat16)


def with_ends(entries, own_key, low, high):
    spot = [jax.random.randint(jax.random.fold_in(own_key, axis), (), 0, length) for axis, length in enumerate(entries.shape)]
    main_axis = entries.shape.index(max(entries.shape))
    neighbour = spot[:main_axis] + [(spot[main_axis] + 1) % entries.shape[main_axis]] + spot[main_axis + 1:]
    return entries.at[tuple(spot)].set(low).at[tuple(neighbour)].set(high)


def levels(stream_key, dims, cuts, smallest, top_value):
    level = 1.0
    for dim, parts in cuts:
        steps = jax.random.uniform(jax.random.fold_in(jax.random.fold_in(stream_key, 6), dim), (parts,), jnp.float32, smallest / len(cuts), top_value / len(cuts))
        level = level * jnp.repeat(jnp.exp(steps), dims[dim] // parts).reshape((-1,) + (1,) * (len(dims) - 1 - dim))
    return level


def routed_block(own_key, own, number, rows, amount, top, bound, skew):
    sequence = jax.random.permutation(own_key, amount)
    packed, usual = load_shares(amount, rows * top, bound, skew, True), load_shares(amount, rows * top, bound, skew, False)
    places = jnp.arange(amount)

    def named(sizes, turn):
        used = int((sizes > 0).sum())
        fixed = max(1, used // 4)
        passed = fixed + (places - fixed + turn * (used - fixed)) % max(1, amount - fixed)
        return jnp.zeros((amount,), jnp.int32).at[sequence[jnp.where(places < fixed, places, passed)]].set(jnp.asarray(sizes, jnp.int32))

    sizes = jnp.where(number % 4 == 0, named(packed, number // 4), named(usual, number - number // 4 - 1))
    mixed = jax.random.permutation(jax.random.fold_in(own, 3), amount)
    donor, receiver = mixed[0:amount // 2 * 2:2], mixed[1:amount // 2 * 2:2]
    margin = jnp.minimum(sizes[donor] - 1, bound - sizes[receiver]) // 2
    margin = jnp.where((donor == sequence[0]) | (receiver == sequence[0]) | (sizes[receiver] == 0), 0, jnp.maximum(margin, 0))
    passed = jax.random.randint(jax.random.fold_in(own, 4), (amount // 2,), 0, 1 << 20) % (margin + 1)
    sizes = sizes.at[donor].add(-passed).at[receiver].add(passed)
    members = jnp.searchsorted(jnp.cumsum(sizes), jnp.arange(rows * top), side="right").astype(jnp.int32)
    listing = members.reshape(top, rows).T
    listing = listing[jax.random.permutation(jax.random.fold_in(own, 1), rows)]
    turn = jax.random.randint(jax.random.fold_in(own, 2), (rows, 1), 0, top)
    return jnp.take_along_axis(listing, (jnp.arange(top)[None, :] + turn) % top, axis=1)


def load_shares(count, total, bound, slope, full):
    portions = [(1 << 20) // math.isqrt(standing ** slope) + 1 for standing in range(1, count + 1)]
    largest = bound if full else min(bound, max(-(-total // count), total * portions[0] // sum(portions)))
    least = 1 if total - largest >= count - 1 else 0
    holding, surplus = [largest] + [least] * (count - 1), total - largest - least * (count - 1)
    while surplus > 0:
        candidates = [i for i in range(1, count) if holding[i] < largest] or [i for i in range(1, count) if holding[i] < bound]
        mass, left = sum([portions[i] for i in candidates]), surplus
        for i in candidates:
            extra = min(bound - holding[i], max(1, left * portions[i] // mass), surplus)
            holding[i] = holding[i] + extra
            surplus = surplus - extra
    return np.array(holding)


def noise(own_key, dims, width, most, pieces=(), held_as=jnp.bfloat16):
    array = width * jax.random.normal(own_key, dims, jnp.float32)
    if pieces:
        array = array * levels(own_key, dims, pieces, -0.22, 0.18)
    return jnp.clip(array, -most, most).astype(held_as)


def setup_inputs(seed: int = 0) -> dict:
    key_of = jax.random.split(jax.random.key(seed), 9)
    queries = draw_queries(jax.random.fold_in(key_of[8], 71), 0)
    grad_out = noise(key_of[1], (ROWS, SEG, HEADS * HEAD), 1.0, 6.0, ((0, 64), (2, 8)))
    image_keys = draw_image_keys(jax.random.fold_in(key_of[8], 71), 0)
    image_values = noise(key_of[3], (IMAGES, KEYS, KV_HEADS * HEAD), 1.0, 6.0, ((0, 64), (2, 8)))
    gate_logits = jnp.clip(jax.random.uniform(key_of[4], (HEADS,), jnp.float32, -1.5, 1.5) * levels(key_of[4], (HEADS,), ((0, 8),), -0.4, 0.0), -1.5, 1.5)
    tile_counts = with_ends(jax.random.randint(key_of[5], (IMAGES,), 1, TILES_MAX + 1), jax.random.fold_in(key_of[5], 1), 1, TILES_MAX).astype(jnp.int32)
    owners_keys = jax.random.split(jax.random.fold_in(key_of[6], 1), ROWS // ROWS_DEV)
    owners_turns = jax.random.permutation(jax.random.fold_in(key_of[6], 3), ROWS // ROWS_DEV)
    owners = jax.vmap(lambda own, number: routed_block(jax.random.fold_in(key_of[6], 2), own, number, ROWS_DEV, IMAGES, 1, CAP, 2))(owners_keys, owners_turns).reshape((ROWS, 1))
    text_only = with_ends((jax.random.randint(key_of[7], (ROWS,), 0, 5) < 2).astype(jnp.int32), jax.random.fold_in(key_of[7], 1), 0, 1)
    return dict(queries=queries, grad_out=grad_out, image_keys=image_keys, image_values=image_values, gate_logits=gate_logits, tile_counts=tile_counts, owners=owners, text_only=text_only)


def reference(queries, grad_out, image_keys, image_values, gate_logits, tile_counts, owners, text_only):
    row_total = queries.shape[0]
    group_size = HEADS // KV_HEADS
    score_scale = HEAD ** -0.5
    row_block = 16
    head_gate = jnp.tanh(gate_logits).reshape(KV_HEADS, group_size)[None, :, :, None, None]
    key_index = jnp.arange(KEYS, dtype=jnp.int32)
    owner_list = owners[:, 0]
    highest = lax.Precision.HIGHEST

    def one_block(running, block_id):
        grad_key, grad_value = running
        block_start = (block_id * row_block).astype(jnp.int32)
        query_block = lax.dynamic_slice_in_dim(queries, block_start, row_block, 0).astype(jnp.float32)
        query_block = query_block.reshape(row_block, SEG, KV_HEADS, group_size, HEAD)
        grad_block = lax.dynamic_slice_in_dim(grad_out, block_start, row_block, 0).astype(jnp.float32)
        grad_block = grad_block.reshape(row_block, SEG, KV_HEADS, group_size, HEAD)
        target = lax.dynamic_slice_in_dim(owner_list, block_start, row_block, 0).astype(jnp.int32)
        live_rows = (1 - lax.dynamic_slice_in_dim(text_only, block_start, row_block, 0)).astype(jnp.float32)
        key_block = image_keys[target].astype(jnp.float32).reshape(row_block, KEYS, KV_HEADS, HEAD)
        value_block = image_values[target].astype(jnp.float32).reshape(row_block, KEYS, KV_HEADS, HEAD)
        limit = tile_counts[target] * TILE
        key_live = key_index[None, :] < limit[:, None]
        scores = jnp.einsum("bsngd,bknd->bngsk", query_block, key_block, precision=highest) * score_scale
        scores = jnp.where(key_live[:, None, None, None, :], scores, -1e30)
        largest = jnp.max(scores, axis=-1, keepdims=True)
        expo_terms = jnp.exp(scores - largest)
        probs = expo_terms / jnp.sum(expo_terms, axis=-1, keepdims=True)
        weighted = (head_gate * probs).astype(jnp.bfloat16)
        grad_probs = jnp.einsum("bsngd,bknd->bngsk", grad_block, value_block, precision=highest)
        row_delta = jnp.sum(probs * grad_probs, axis=-1, keepdims=True)
        grad_scores = (probs * (grad_probs - row_delta) * head_gate * score_scale).astype(jnp.bfloat16)
        grad_query = jnp.einsum("bngsk,bknd->bsngd", grad_scores.astype(jnp.float32), key_block, precision=highest)
        grad_query = grad_query * live_rows[:, None, None, None, None]
        grad_query = grad_query.astype(jnp.bfloat16).reshape(row_block, SEG, HEADS * HEAD)
        key_part = jnp.einsum("bngsk,bsngd->bknd", grad_scores.astype(jnp.float32), query_block, precision=highest)
        value_part = jnp.einsum("bngsk,bsngd->bknd", weighted.astype(jnp.float32), grad_block, precision=highest)
        key_part = (key_part * live_rows[:, None, None, None]).reshape(row_block, KEYS, KV_HEADS * HEAD)
        value_part = (value_part * live_rows[:, None, None, None]).reshape(row_block, KEYS, KV_HEADS * HEAD)
        grad_key = grad_key.at[target].add(key_part)
        grad_value = grad_value.at[target].add(value_part)
        return (grad_key, grad_value), grad_query

    initial = (jnp.zeros((IMAGES, KEYS, KV_HEADS * HEAD), jnp.float32),
               jnp.zeros((IMAGES, KEYS, KV_HEADS * HEAD), jnp.float32))
    finals, grad_rows = lax.scan(one_block, initial, jnp.arange(row_total // row_block, dtype=jnp.int32))
    grad_queries = grad_rows.reshape(row_total, SEG, HEADS * HEAD)
    return grad_queries, finals[0].astype(jnp.bfloat16), finals[1].astype(jnp.bfloat16)
```

```python
import math

import jax
import jax.numpy as jnp
from jax import lax
from jax.experimental import pallas as pl
from jax.experimental.pallas import tpu as pltpu
from jax.sharding import PartitionSpec as P

HEAD = 128
TILE = 256
CAP = 3
SUB = 256
GROUP = 16
SCALE = HEAD ** (-0.5)


def pack_kernel(
    owner_hbm, text_hbm, query_hbm, grad_hbm, send_hbm, slot_ref,
    owners, texts, count, place_of, query_rows, grad_rows, query_slots, grad_slots,
    in_sems, out_sems,
):
    rows = query_rows.shape[0]
    peers = query_slots.shape[0] - 1
    owner_copy = pltpu.make_async_copy(owner_hbm, owners, in_sems.at[0])
    text_copy = pltpu.make_async_copy(text_hbm, texts, in_sems.at[1])
    query_copy = pltpu.make_async_copy(query_hbm, query_rows, in_sems.at[2])
    grad_copy = pltpu.make_async_copy(grad_hbm, grad_rows, in_sems.at[3])
    owner_copy.start()
    text_copy.start()
    query_copy.start()
    grad_copy.start()
    for peer in range(peers):
        count[peer] = 0
    query_slots[...] = jnp.zeros(query_slots.shape, query_slots.dtype)
    grad_slots[...] = jnp.zeros(grad_slots.shape, grad_slots.dtype)
    owner_copy.wait()
    text_copy.wait()

    @pl.loop(0, rows // 8)
    def _(group):
        for inner in range(8):
            row = group * 8 + inner
            owner = owners[row]
            live = texts[row] == 0
            rank = count[owner]
            count[owner] = rank + jnp.where(live, 1, 0)
            place_of[row] = jnp.where(live, owner * 4 + rank, peers * 4)
            slot_ref[row] = jnp.where(live, owner * CAP + rank, -1)

    out_copies = []
    for which, (copy, source, target) in enumerate(
        ((query_copy, query_rows, query_slots), (grad_copy, grad_rows, grad_slots))
    ):
        copy.wait()

        @pl.loop(0, rows // 8)
        def _(group, source=source, target=target):
            for inner in range(8):
                row = group * 8 + inner
                place = place_of[row]
                target[place >> 2, place & 3] = source[row]

        out = pltpu.make_async_copy(
            target.at[pl.ds(0, peers)],
            send_hbm.at[:, pl.ds(which * CAP, CAP)],
            out_sems.at[which],
        )
        out.start()
        out_copies.append(out)
    for out in out_copies:
        out.wait()


def pack(owners, text_only, queries, grad_out, peers):
    rows = queries.shape[0]
    slab = queries.shape[1:]
    hbm = pl.BlockSpec(memory_space=pltpu.HBM)
    padded = (peers + 1, CAP) + slab
    return pl.pallas_call(
        pack_kernel,
        out_shape=(
            jax.ShapeDtypeStruct((peers, 2 * CAP) + slab, jnp.bfloat16),
            jax.ShapeDtypeStruct((rows,), jnp.int32),
        ),
        in_specs=[hbm, hbm, hbm, hbm],
        out_specs=(hbm, pl.BlockSpec(memory_space=pltpu.SMEM)),
        scratch_shapes=[
            pltpu.SMEM((rows,), jnp.int32),
            pltpu.SMEM((rows,), jnp.int32),
            pltpu.SMEM((peers,), jnp.int32),
            pltpu.SMEM((rows,), jnp.int32),
            pltpu.VMEM((rows,) + slab, jnp.bfloat16),
            pltpu.VMEM((rows,) + slab, jnp.bfloat16),
            pltpu.VMEM(padded, jnp.bfloat16),
            pltpu.VMEM(padded, jnp.bfloat16),
            pltpu.SemaphoreType.DMA((4,)),
            pltpu.SemaphoreType.DMA((2,)),
        ],
        compiler_params=pltpu.CompilerParams(vmem_limit_bytes=60 * 2**20),
        name="pack_rows",
    )(owners, text_only, queries, grad_out)


def unpack_kernel(slot_ref, slots_ref, out_hbm, rows_ref, sems):
    rows = rows_ref.shape[0]
    parts = sems.shape[0]
    share = rows // parts
    copies = []
    for part in range(parts):
        @pl.loop(0, share // 8)
        def _(group, part=part):
            for inner in range(8):
                row = part * share + group * 8 + inner
                slot = slot_ref[row]
                slab = slots_ref[jnp.maximum(slot, 0)]
                rows_ref[row] = jnp.where(slot >= 0, slab, jnp.zeros_like(slab))

        piece = pl.ds(part * share, share)
        copy = pltpu.make_async_copy(rows_ref.at[piece], out_hbm.at[piece], sems.at[part])
        copy.start()
        copies.append(copy)
    for copy in copies:
        copy.wait()


def unpack(slot_of, slots):
    rows = (slot_of.shape[0],) + slots.shape[1:]
    return pl.pallas_call(
        unpack_kernel,
        out_shape=jax.ShapeDtypeStruct(rows, jnp.bfloat16),
        in_specs=[pl.BlockSpec(memory_space=pltpu.SMEM), pl.BlockSpec(memory_space=pltpu.VMEM)],
        out_specs=pl.BlockSpec(memory_space=pltpu.HBM),
        scratch_shapes=[pltpu.VMEM(rows, jnp.bfloat16), pltpu.SemaphoreType.DMA((4,))],
        compiler_params=pltpu.CompilerParams(vmem_limit_bytes=48 * 2**20),
        name="unpack_rows",
    )(slot_of, slots)


def nt_dot(a, b):
    return lax.dot_general(a, b, (((1,), (1,)), ((), ())), preferred_element_type=jnp.float32)


def nn_dot(a, b):
    return jnp.dot(a, b, preferred_element_type=jnp.float32)


def softmax_terms(keys, values, query, grad):
    scores = nt_dot(keys, query)
    top = jnp.max(scores, axis=0, keepdims=True)
    expo = jnp.exp2((scores - top) * (SCALE * math.log2(math.e)))
    total = jnp.sum(expo, axis=0, keepdims=True)
    grad_probs = nt_dot(values, grad)
    delta = jnp.sum(expo * grad_probs, axis=0, keepdims=True) / total
    return expo, total, grad_probs, delta


def gather_block(block, place_ref, received, query_cols, grad_cols):
    for lane in range(GROUP):
        place = place_ref[block * GROUP + lane]
        query_cols[lane * 32:lane * 32 + 32] = received[place]
        grad_cols[lane * 32:lane * 32 + 32] = received[place + CAP]


def query_grad_kernel(
    tiles_ref, gate_ref, key_ref, value_ref, turned_ref, received,
    out_ref, place_ref, blocks_ref,
    slot_list, query_cols, grad_cols,
):
    slots = out_ref.shape[0]
    out_ref[...] = jnp.zeros(out_ref.shape, out_ref.dtype)
    found = jnp.int32(0)
    spare = jnp.int32(0)
    for slot in range(slots):
        place = slot // CAP * (2 * CAP) + slot % CAP
        slab = jnp.abs(received[place + CAP].astype(jnp.float32))
        live = jnp.max(slab) > 0.0
        place_ref[found] = jnp.int32(place)
        slot_list[found] = jnp.int32(slot)
        spare = jnp.where(live, spare, slot)
        found = found + jnp.where(live, 1, 0)
    blocks = (found + (GROUP - 1)) // GROUP
    blocks_ref[0] = blocks
    spare_place = spare // CAP * (2 * CAP) + spare % CAP
    for extra in range(GROUP):
        place_ref[found + extra] = spare_place
        slot_list[found + extra] = spare

    def work(live):
        @pl.loop(0, blocks)
        def _(block):
            gather_block(block, place_ref, received, query_cols, grad_cols)
            for start in range(0, GROUP * 32, SUB):
                query = query_cols[start:start + SUB]
                grad = grad_cols[start:start + SUB]
                expo, total, grad_probs, delta = softmax_terms(
                    key_ref[:live], value_ref[:live], query, grad
                )
                weighted = expo * (gate_ref[...] / total)
                score_grad = (weighted * (grad_probs - delta)).astype(jnp.bfloat16)
                turned = nn_dot(turned_ref[:, :live], score_grad) * SCALE
                slabs = turned.T.astype(jnp.bfloat16).reshape(SUB // 32, 32, HEAD)
                for lane in range(SUB // 32):
                    out_ref[slot_list[block * GROUP + start // 32 + lane]] = slabs[lane]

    most = key_ref.shape[0] // TILE
    for count in range(1, most + 1):
        @pl.when(tiles_ref[0] == count)
        def _(count=count):
            work(count * TILE)


def query_grads(tile_counts, gate, key_rows, value_rows, key_turned, received):
    slots = received.shape[0] // 2
    smem = pl.BlockSpec(memory_space=pltpu.SMEM)
    vmem = pl.BlockSpec(memory_space=pltpu.VMEM)
    return pl.pallas_call(
        query_grad_kernel,
        out_shape=(
            jax.ShapeDtypeStruct((slots, 32, HEAD), jnp.bfloat16),
            jax.ShapeDtypeStruct((slots + GROUP,), jnp.int32),
            jax.ShapeDtypeStruct((1,), jnp.int32),
        ),
        in_specs=[smem, vmem, vmem, vmem, vmem, vmem],
        out_specs=(vmem, smem, smem),
        scratch_shapes=[
            pltpu.SMEM((slots + GROUP,), jnp.int32),
            pltpu.VMEM((GROUP * 32, HEAD), jnp.bfloat16),
            pltpu.VMEM((GROUP * 32, HEAD), jnp.bfloat16),
        ],
        compiler_params=pltpu.CompilerParams(vmem_limit_bytes=40 * 2**20),
        name="query_grads",
    )(tile_counts, gate, key_rows, value_rows, key_turned, received)


def image_grad_kernel(
    tiles_ref, place_ref, blocks_ref, gate_ref, key_ref, value_ref, received,
    grad_key_ref, grad_value_ref,
    key_sum, value_sum, query_cols, grad_cols, score_grads, weights,
):
    key_sum[...] = jnp.zeros(key_sum.shape, jnp.float32)
    value_sum[...] = jnp.zeros(value_sum.shape, jnp.float32)

    def work(live):
        @pl.loop(0, blocks_ref[0])
        def _(block):
            gather_block(block, place_ref, received, query_cols, grad_cols)
            for start in range(0, GROUP * 32, SUB):
                part = pl.ds(start, SUB)
                expo, total, grad_probs, delta = softmax_terms(
                    key_ref[:live], value_ref[:live],
                    query_cols[start:start + SUB], grad_cols[start:start + SUB],
                )
                weighted = expo * (gate_ref[...] / total)
                weights[:live, part] = weighted.astype(jnp.bfloat16)
                score_grads[:live, part] = (weighted * (grad_probs - delta)).astype(jnp.bfloat16)
            key_sum[:live] += nn_dot(score_grads[:live], query_cols[...])
            value_sum[:live] += nn_dot(weights[:live], grad_cols[...])

    most = key_ref.shape[0] // TILE
    for count in range(1, most + 1):
        @pl.when(tiles_ref[0] == count)
        def _(count=count):
            work(count * TILE)

    grad_key_ref[...] = (key_sum[...] * SCALE).astype(jnp.bfloat16)
    grad_value_ref[...] = value_sum[...].astype(jnp.bfloat16)


def image_grads(tile_counts, places, blocks, gate, key_rows, value_rows, received):
    keys = key_rows.shape[0]
    cols = GROUP * 32
    smem = pl.BlockSpec(memory_space=pltpu.SMEM)
    vmem = pl.BlockSpec(memory_space=pltpu.VMEM)
    return pl.pallas_call(
        image_grad_kernel,
        out_shape=(
            jax.ShapeDtypeStruct((keys, HEAD), jnp.bfloat16),
            jax.ShapeDtypeStruct((keys, HEAD), jnp.bfloat16),
        ),
        in_specs=[smem, smem, smem, vmem, vmem, vmem, vmem],
        out_specs=(vmem, vmem),
        scratch_shapes=[
            pltpu.VMEM((keys, HEAD), jnp.float32),
            pltpu.VMEM((keys, HEAD), jnp.float32),
            pltpu.VMEM((cols, HEAD), jnp.bfloat16),
            pltpu.VMEM((cols, HEAD), jnp.bfloat16),
            pltpu.VMEM((keys, cols), jnp.bfloat16),
            pltpu.VMEM((keys, cols), jnp.bfloat16),
        ],
        compiler_params=pltpu.CompilerParams(vmem_limit_bytes=40 * 2**20),
        cost_estimate=pl.CostEstimate(
            flops=8 * received.shape[0] * 16 * keys * HEAD,
            bytes_accessed=4 * 2**20,
            transcendentals=received.shape[0] * 16 * keys,
        ),
        name="image_grads",
    )(tile_counts, places, blocks, gate, key_rows, value_rows, received)


def on_device(
    queries, grad_out, image_keys, image_values, gate_logits, tile_counts, owners, text_only
):
    rows, tokens, width = queries.shape
    heads = width // HEAD
    peers = lax.axis_size("dp")

    def slabs(array):
        split = array.reshape(rows, tokens, heads, HEAD).transpose(0, 2, 1, 3)
        return split.reshape(rows, heads * tokens, HEAD)

    send, slot_of = pack(owners[:, 0], text_only, slabs(queries), slabs(grad_out), peers)
    received = lax.all_to_all(send, "dp", split_axis=0, concat_axis=0, tiled=True)
    received = received.reshape(peers * 2 * CAP, heads * tokens, HEAD)
    key_rows, value_rows = image_keys[0], image_values[0]
    gate = jnp.tile(jnp.repeat(jnp.tanh(gate_logits), tokens), SUB // 32)[None]
    grad_slots, places, blocks = query_grads(
        tile_counts, gate, key_rows, value_rows, key_rows.T, received
    )
    returned = lax.all_to_all(
        grad_slots.reshape(peers, CAP, heads * tokens, HEAD),
        "dp", split_axis=0, concat_axis=0, tiled=True,
    )
    grad_key, grad_value = image_grads(
        tile_counts, places, blocks, gate, key_rows, value_rows, received
    )
    grad_rows = unpack(slot_of, returned.reshape(peers * CAP, heads * tokens, HEAD))
    grad_rows = grad_rows.reshape(rows, heads, tokens, HEAD).transpose(0, 2, 1, 3)
    return grad_rows.reshape(rows, tokens, width), grad_key[None], grad_value[None]


def solution(mesh):
    placed = (
        P("dp", None, "tensor"),
        P("dp", None, "tensor"),
        P("dp", None, "tensor"),
        P("dp", None, "tensor"),
        P("tensor"),
        P("dp"),
        P("dp", None),
        P("dp"),
    )
    return jax.shard_map(
        on_device,
        mesh=mesh,
        in_specs=placed,
        out_specs=(P("dp", None, "tensor"), P("dp", None, "tensor"), P("dp", None, "tensor")),
        check_vma=False,
    )
```

```python
import math

import jax
import jax.numpy as jnp
from jax import lax
from jax.experimental import pallas as pl
from jax.experimental.pallas import tpu as pltpu
from jax.sharding import PartitionSpec as P

HEAD = 128
TILE = 256
CAP = 3
SUB = 256
GROUP = 16
CHUNK = 128
PIECES = 4
SCALE = HEAD ** (-0.5)


def pack_kernel(
    owner_hbm, text_hbm, query_hbm, grad_hbm, send_hbm, slot_ref,
    owners, texts, count, place_of, query_rows, grad_rows, query_slots, grad_slots,
    in_sems, out_sems,
):
    rows = query_rows.shape[0]
    peers = query_slots.shape[0] - 1
    owner_copy = pltpu.make_async_copy(owner_hbm, owners, in_sems.at[0])
    text_copy = pltpu.make_async_copy(text_hbm, texts, in_sems.at[1])
    query_copy = pltpu.make_async_copy(query_hbm, query_rows, in_sems.at[2])
    grad_copy = pltpu.make_async_copy(grad_hbm, grad_rows, in_sems.at[3])
    owner_copy.start()
    text_copy.start()
    query_copy.start()
    grad_copy.start()
    for peer in range(peers):
        count[peer] = 0
    query_slots[...] = jnp.zeros(query_slots.shape, query_slots.dtype)
    grad_slots[...] = jnp.full(grad_slots.shape, jnp.inf, grad_slots.dtype)
    owner_copy.wait()
    text_copy.wait()

    @pl.loop(0, rows // 8)
    def _(group):
        for inner in range(8):
            row = group * 8 + inner
            owner = owners[row]
            live = texts[row] == 0
            rank = count[owner]
            count[owner] = rank + jnp.where(live, 1, 0)
            place_of[row] = jnp.where(live, owner * 4 + rank, peers * 4)
            slot_ref[row] = jnp.where(live, owner * CAP + rank, -1)

    out_copies = []
    for which, (copy, source, target) in enumerate(
        ((query_copy, query_rows, query_slots), (grad_copy, grad_rows, grad_slots))
    ):
        copy.wait()

        @pl.loop(0, rows // 8)
        def _(group, source=source, target=target):
            for inner in range(8):
                row = group * 8 + inner
                place = place_of[row]
                target[place >> 2, place & 3] = source[row]

        out = pltpu.make_async_copy(
            target.at[pl.ds(0, peers)],
            send_hbm.at[:, pl.ds(which * CAP, CAP)],
            out_sems.at[which],
        )
        out.start()
        out_copies.append(out)
    for out in out_copies:
        out.wait()


def pack(owners, text_only, queries, grad_out, peers):
    rows = queries.shape[0]
    slab = queries.shape[1:]
    hbm = pl.BlockSpec(memory_space=pltpu.HBM)
    padded = (peers + 1, CAP) + slab
    return pl.pallas_call(
        pack_kernel,
        out_shape=(
            jax.ShapeDtypeStruct((peers, 2 * CAP) + slab, jnp.bfloat16),
            jax.ShapeDtypeStruct((rows,), jnp.int32),
        ),
        in_specs=[hbm, hbm, hbm, hbm],
        out_specs=(hbm, pl.BlockSpec(memory_space=pltpu.SMEM)),
        scratch_shapes=[
            pltpu.SMEM((rows,), jnp.int32),
            pltpu.SMEM((rows,), jnp.int32),
            pltpu.SMEM((peers,), jnp.int32),
            pltpu.SMEM((rows,), jnp.int32),
            pltpu.VMEM((rows,) + slab, jnp.bfloat16),
            pltpu.VMEM((rows,) + slab, jnp.bfloat16),
            pltpu.VMEM(padded, jnp.bfloat16),
            pltpu.VMEM(padded, jnp.bfloat16),
            pltpu.SemaphoreType.DMA((4,)),
            pltpu.SemaphoreType.DMA((2,)),
        ],
        compiler_params=pltpu.CompilerParams(vmem_limit_bytes=60 * 2**20),
        name="pack_rows",
    )(owners, text_only, queries, grad_out)


def unpack_kernel(slot_ref, slots_ref, out_hbm, rows_ref, sems):
    rows = rows_ref.shape[0]
    parts = sems.shape[0]
    share = rows // parts
    copies = []
    for part in range(parts):
        @pl.loop(0, share // 8)
        def _(group, part=part):
            for inner in range(8):
                row = part * share + group * 8 + inner
                slot = slot_ref[row]
                slab = slots_ref[jnp.maximum(slot, 0)]
                rows_ref[row] = jnp.where(slot >= 0, slab, jnp.zeros_like(slab))

        piece = pl.ds(part * share, share)
        copy = pltpu.make_async_copy(rows_ref.at[piece], out_hbm.at[piece], sems.at[part])
        copy.start()
        copies.append(copy)
    for copy in copies:
        copy.wait()


def unpack(slot_of, slots):
    rows = (slot_of.shape[0],) + slots.shape[1:]
    return pl.pallas_call(
        unpack_kernel,
        out_shape=jax.ShapeDtypeStruct(rows, jnp.bfloat16),
        in_specs=[pl.BlockSpec(memory_space=pltpu.SMEM), pl.BlockSpec(memory_space=pltpu.VMEM)],
        out_specs=pl.BlockSpec(memory_space=pltpu.HBM),
        scratch_shapes=[pltpu.VMEM(rows, jnp.bfloat16), pltpu.SemaphoreType.DMA((4,))],
        compiler_params=pltpu.CompilerParams(vmem_limit_bytes=48 * 2**20),
        name="unpack_rows",
    )(slot_of, slots)


def nt_dot(a, b):
    return lax.dot_general(a, b, (((1,), (1,)), ((), ())), preferred_element_type=jnp.float32)


def nn_dot(a, b):
    return jnp.dot(a, b, preferred_element_type=jnp.float32)


def softmax_terms(key_value_ref, live, query, grad, gate):
    keys = key_value_ref.shape[0] // 2
    cols = query.shape[0]
    scores = nt_dot(key_value_ref[:live], query)
    grad_probs = nt_dot(key_value_ref[keys:keys + live], grad)
    tops, expos, grads, sums, dots = [], [], [], [], []
    for start in range(0, live, CHUNK):
        score = scores[start:start + CHUNK].reshape(CHUNK // 8, 8, cols)
        top = jnp.max(score, axis=0)
        expo = jnp.exp2((score - top) * (SCALE * math.log2(math.e)))
        grad_prob = grad_probs[start:start + CHUNK].reshape(CHUNK // 8, 8, cols)
        tops.append(top)
        expos.append(expo)
        grads.append(grad_prob)
        sums.append(jnp.sum(expo, axis=0))
        dots.append(jnp.sum(expo * grad_prob, axis=0))
    largest = tops[0]
    for top in tops[1:]:
        largest = jnp.maximum(largest, top)
    largest = jnp.max(largest, axis=0, keepdims=True)
    factors = [jnp.exp2((top - largest) * (SCALE * math.log2(math.e))) for top in tops]
    total = sum(factor * part for factor, part in zip(factors, sums))
    delta = sum(factor * part for factor, part in zip(factors, dots))
    inverse = 1.0 / jnp.sum(total, axis=0, keepdims=True)
    delta = jnp.sum(delta, axis=0, keepdims=True) * inverse
    factors = [factor * (inverse * gate) for factor in factors]
    return expos, grads, factors, jnp.broadcast_to(delta, (8, cols))


def gather_block(block, found, place_ref, received, query_cols, grad_cols):
    for lane in range(GROUP):
        index = block * GROUP + lane
        place = place_ref[index]
        grad = received[place + CAP]
        query_cols[lane * 32:lane * 32 + 32] = received[place]
        grad_cols[lane * 32:lane * 32 + 32] = jnp.where(index < found, grad, jnp.zeros_like(grad))


def query_grad_kernel(
    tiles_ref, gate_ref, key_value_hbm, turned_hbm, received_hbm,
    out_hbm, place_ref, found_ref,
    slot_list, key_value_ref, turned_ref, received,
    query_cols, grad_cols, score_grads, out_slots, in_sems, out_sem,
):
    slots = out_hbm.shape[0]
    peers = slots // CAP
    share = received.shape[0] // PIECES
    in_copies = []
    for number in range(PIECES):
        piece = pl.ds(number * share, share)
        in_copies.append(pltpu.make_async_copy(
            received_hbm.at[piece], received.at[piece], in_sems.at[number]
        ))
    key_copy = pltpu.make_async_copy(key_value_hbm, key_value_ref, in_sems.at[PIECES])
    turned_copy = pltpu.make_async_copy(turned_hbm, turned_ref, in_sems.at[PIECES + 1])
    for copy in in_copies:
        copy.start()
    key_copy.start()
    turned_copy.start()
    found = jnp.int32(0)
    for peer in range(peers):
        if peer % (peers // PIECES) == 0:
            in_copies[peer // (peers // PIECES)].wait()
        used = jnp.zeros((16, HEAD), jnp.float32)
        for rank in range(CAP):
            first = received[peer * 2 * CAP + CAP + rank, 0:16].astype(jnp.float32)
            used = used + jnp.where(first < jnp.inf, 1.0, 0.0)
            place_ref[found + rank] = jnp.int32(peer * 2 * CAP + rank)
            slot_list[found + rank] = jnp.int32(peer * CAP + rank)
        found = found + used[0, 0].astype(jnp.int32)
    found_ref[0] = found
    for extra in range(GROUP):
        place_ref[found + extra] = jnp.int32(0)
        slot_list[found + extra] = jnp.int32(slots)
    key_copy.wait()
    turned_copy.wait()

    def work(live):
        @pl.loop(0, (found + (GROUP - 1)) // GROUP)
        def _(block):
            gather_block(block, found, place_ref, received, query_cols, grad_cols)
            for start in range(0, GROUP * 32, SUB):
                expos, grads, factors, delta = softmax_terms(
                    key_value_ref, live,
                    query_cols[start:start + SUB], grad_cols[start:start + SUB], gate_ref[...],
                )
                for number, (expo, grad, factor) in enumerate(zip(expos, grads, factors)):
                    score_grad = expo * factor * (grad - delta)
                    score_grads[number * CHUNK:(number + 1) * CHUNK, start:start + SUB] = (
                        score_grad.reshape(CHUNK, SUB).astype(jnp.bfloat16)
                    )
                turned = nn_dot(turned_ref[:, :live], score_grads[:live, start:start + SUB])
                slabs = (turned * SCALE).T.astype(jnp.bfloat16).reshape(SUB // 32, 32, HEAD)
                for lane in range(SUB // 32):
                    out_slots[slot_list[block * GROUP + start // 32 + lane]] = slabs[lane]

    most = key_value_ref.shape[0] // 2 // TILE
    for count in range(1, most + 1):
        @pl.when(tiles_ref[0] == count)
        def _(count=count):
            work(count * TILE)

    out = pltpu.make_async_copy(out_slots.at[pl.ds(0, slots)], out_hbm, out_sem)
    out.start()
    out.wait()


def query_grads(tile_counts, gate, key_values, key_turned, received):
    slots = received.shape[0] // 2
    keys = key_values.shape[0] // 2
    cols = GROUP * 32
    smem = pl.BlockSpec(memory_space=pltpu.SMEM)
    hbm = pl.BlockSpec(memory_space=pltpu.HBM)
    vmem = pl.BlockSpec(memory_space=pltpu.VMEM)
    return pl.pallas_call(
        query_grad_kernel,
        out_shape=(
            jax.ShapeDtypeStruct((slots, 32, HEAD), jnp.bfloat16),
            jax.ShapeDtypeStruct((slots + GROUP,), jnp.int32),
            jax.ShapeDtypeStruct((1,), jnp.int32),
        ),
        in_specs=[smem, vmem, hbm, hbm, hbm],
        out_specs=(hbm, smem, smem),
        scratch_shapes=[
            pltpu.SMEM((slots + GROUP,), jnp.int32),
            pltpu.VMEM(key_values.shape, jnp.bfloat16),
            pltpu.VMEM(key_turned.shape, jnp.bfloat16),
            pltpu.VMEM(received.shape, jnp.bfloat16),
            pltpu.VMEM((cols, HEAD), jnp.bfloat16),
            pltpu.VMEM((cols, HEAD), jnp.bfloat16),
            pltpu.VMEM((keys, cols), jnp.bfloat16),
            pltpu.VMEM((slots + 1, 32, HEAD), jnp.bfloat16),
            pltpu.SemaphoreType.DMA((PIECES + 2,)),
            pltpu.SemaphoreType.DMA,
        ],
        compiler_params=pltpu.CompilerParams(vmem_limit_bytes=60 * 2**20),
        name="query_grads",
    )(tile_counts, gate, key_values, key_turned, received)


def image_grad_kernel(
    tiles_ref, place_ref, found_ref, gate_ref, key_value_ref, received,
    grad_key_ref, grad_value_ref,
    key_sum, value_sum, query_cols, grad_cols, score_grads, weights,
):
    found = found_ref[0]
    key_sum[...] = jnp.zeros(key_sum.shape, jnp.float32)
    value_sum[...] = jnp.zeros(value_sum.shape, jnp.float32)

    def work(live):
        @pl.loop(0, (found + (GROUP - 1)) // GROUP)
        def _(block):
            gather_block(block, found, place_ref, received, query_cols, grad_cols)
            for start in range(0, GROUP * 32, SUB):
                expos, grads, factors, delta = softmax_terms(
                    key_value_ref, live,
                    query_cols[start:start + SUB], grad_cols[start:start + SUB], gate_ref[...],
                )
                for number, (expo, grad, factor) in enumerate(zip(expos, grads, factors)):
                    rows = slice(number * CHUNK, (number + 1) * CHUNK)
                    weighted = expo * factor
                    score_grad = weighted * (grad - delta)
                    weights[rows, start:start + SUB] = (
                        weighted.reshape(CHUNK, SUB).astype(jnp.bfloat16)
                    )
                    score_grads[rows, start:start + SUB] = (
                        score_grad.reshape(CHUNK, SUB).astype(jnp.bfloat16)
                    )
            key_sum[:live] += nn_dot(score_grads[:live], query_cols[...])
            value_sum[:live] += nn_dot(weights[:live], grad_cols[...])

    most = key_value_ref.shape[0] // 2 // TILE
    for count in range(1, most + 1):
        @pl.when(tiles_ref[0] == count)
        def _(count=count):
            work(count * TILE)

    grad_key_ref[...] = (key_sum[...] * SCALE).astype(jnp.bfloat16)
    grad_value_ref[...] = value_sum[...].astype(jnp.bfloat16)


def image_grads(tile_counts, places, found, gate, key_values, received):
    keys = key_values.shape[0] // 2
    cols = GROUP * 32
    smem = pl.BlockSpec(memory_space=pltpu.SMEM)
    vmem = pl.BlockSpec(memory_space=pltpu.VMEM)
    return pl.pallas_call(
        image_grad_kernel,
        out_shape=(
            jax.ShapeDtypeStruct((keys, HEAD), jnp.bfloat16),
            jax.ShapeDtypeStruct((keys, HEAD), jnp.bfloat16),
        ),
        in_specs=[smem, smem, smem, vmem, vmem, vmem],
        out_specs=(vmem, vmem),
        scratch_shapes=[
            pltpu.VMEM((keys, HEAD), jnp.float32),
            pltpu.VMEM((keys, HEAD), jnp.float32),
            pltpu.VMEM((cols, HEAD), jnp.bfloat16),
            pltpu.VMEM((cols, HEAD), jnp.bfloat16),
            pltpu.VMEM((keys, cols), jnp.bfloat16),
            pltpu.VMEM((keys, cols), jnp.bfloat16),
        ],
        compiler_params=pltpu.CompilerParams(vmem_limit_bytes=40 * 2**20),
        cost_estimate=pl.CostEstimate(
            flops=8 * received.shape[0] * 16 * keys * HEAD,
            bytes_accessed=4 * 2**20,
            transcendentals=received.shape[0] * 16 * keys,
        ),
        name="image_grads",
    )(tile_counts, places, found, gate, key_values, received)


def on_device(
    queries, grad_out, image_keys, image_values, gate_logits, tile_counts, owners, text_only
):
    rows, tokens, width = queries.shape
    heads = width // HEAD
    peers = lax.axis_size("dp")

    def slabs(array):
        split = array.reshape(rows, tokens, heads, HEAD).transpose(0, 2, 1, 3)
        return split.reshape(rows, heads * tokens, HEAD)

    send, slot_of = pack(owners[:, 0], text_only, slabs(queries), slabs(grad_out), peers)
    received = lax.all_to_all(send, "dp", split_axis=0, concat_axis=0, tiled=True)
    received = received.reshape(peers * 2 * CAP, heads * tokens, HEAD)
    key_values = jnp.concatenate([image_keys[0], image_values[0]])
    gate = jnp.tile(jnp.repeat(jnp.tanh(gate_logits), tokens), SUB // 32)[None]
    grad_slots, places, found = query_grads(
        tile_counts, gate, key_values, image_keys[0].T, received
    )
    returned = lax.all_to_all(
        grad_slots.reshape(peers, CAP, heads * tokens, HEAD),
        "dp", split_axis=0, concat_axis=0, tiled=True,
    )
    grad_key, grad_value = image_grads(tile_counts, places, found, gate, key_values, received)
    grad_rows = unpack(slot_of, returned.reshape(peers * CAP, heads * tokens, HEAD))
    grad_rows = grad_rows.reshape(rows, heads, tokens, HEAD).transpose(0, 2, 1, 3)
    return grad_rows.reshape(rows, tokens, width), grad_key[None], grad_value[None]


def solution(mesh):
    placed = (
        P("dp", None, "tensor"),
        P("dp", None, "tensor"),
        P("dp", None, "tensor"),
        P("dp", None, "tensor"),
        P("tensor"),
        P("dp"),
        P("dp", None),
        P("dp"),
    )
    return jax.shard_map(
        on_device,
        mesh=mesh,
        in_specs=placed,
        out_specs=(P("dp", None, "tensor"), P("dp", None, "tensor"), P("dp", None, "tensor")),
        check_vma=False,
    )
```

```python
import math

import jax
import jax.numpy as jnp
from jax import lax
from jax.experimental import pallas as pl
from jax.experimental.pallas import tpu as pltpu
from jax.sharding import PartitionSpec as P

HEAD = 128
TILE = 256
CAP = 3
SUB = 256
GROUP = 16
DEPTH = 16
HALVES = 2
CHUNK = 128
SCALE = HEAD ** (-0.5)


def pack_kernel(
    owner_hbm, text_hbm, query_hbm, grad_hbm, send_first, send_second, slot_ref,
    owners, texts, count, place_of, query_rows, grad_rows, query_slots, grad_slots,
    in_sems, out_sems,
):
    rows = query_rows.shape[0]
    peers = query_slots.shape[0] - 1
    send_refs = (send_first, send_second)
    owner_copy = pltpu.make_async_copy(owner_hbm, owners, in_sems.at[0])
    text_copy = pltpu.make_async_copy(text_hbm, texts, in_sems.at[1])
    query_copy = pltpu.make_async_copy(query_hbm, query_rows, in_sems.at[2])
    grad_copy = pltpu.make_async_copy(grad_hbm, grad_rows, in_sems.at[3])
    owner_copy.start()
    text_copy.start()
    query_copy.start()
    grad_copy.start()
    for peer in range(peers):
        count[peer] = 0
    query_slots[...] = jnp.zeros(query_slots.shape, query_slots.dtype)
    grad_slots[...] = jnp.full(grad_slots.shape, jnp.inf, grad_slots.dtype)
    owner_copy.wait()
    text_copy.wait()

    @pl.loop(0, rows // 8)
    def _(group):
        for inner in range(8):
            row = group * 8 + inner
            owner = owners[row]
            live = texts[row] == 0
            rank = count[owner]
            count[owner] = rank + jnp.where(live, 1, 0)
            place_of[row] = jnp.where(live, owner * 4 + rank, peers * 4)
            slot_ref[row] = jnp.where(live, owner * CAP + rank, -1)

    out_copies = []
    for which, (copy, source, target) in enumerate(
        ((query_copy, query_rows, query_slots), (grad_copy, grad_rows, grad_slots))
    ):
        copy.wait()

        @pl.loop(0, rows // 8)
        def _(group, source=source, target=target):
            for inner in range(8):
                row = group * 8 + inner
                place = place_of[row]
                target[place >> 2, place & 3] = source[row]

        for half, send in enumerate(send_refs):
            out = pltpu.make_async_copy(
                target.at[pl.ds(0, peers), :, pl.ds(half * DEPTH, DEPTH)],
                send.at[:, pl.ds(which * CAP, CAP)],
                out_sems.at[which * HALVES + half],
            )
            out.start()
            out_copies.append(out)
    for out in out_copies:
        out.wait()


def pack(owners, text_only, queries, grad_out, peers):
    rows = queries.shape[0]
    slab = queries.shape[1:]
    hbm = pl.BlockSpec(memory_space=pltpu.HBM)
    padded = (peers + 1, CAP) + slab
    return pl.pallas_call(
        pack_kernel,
        out_shape=(
            jax.ShapeDtypeStruct((peers, 2 * CAP, DEPTH, HEAD), jnp.bfloat16),
            jax.ShapeDtypeStruct((peers, 2 * CAP, DEPTH, HEAD), jnp.bfloat16),
            jax.ShapeDtypeStruct((rows,), jnp.int32),
        ),
        in_specs=[hbm, hbm, hbm, hbm],
        out_specs=(hbm, hbm, pl.BlockSpec(memory_space=pltpu.SMEM)),
        scratch_shapes=[
            pltpu.SMEM((rows,), jnp.int32),
            pltpu.SMEM((rows,), jnp.int32),
            pltpu.SMEM((peers,), jnp.int32),
            pltpu.SMEM((rows,), jnp.int32),
            pltpu.VMEM((rows,) + slab, jnp.bfloat16),
            pltpu.VMEM((rows,) + slab, jnp.bfloat16),
            pltpu.VMEM(padded, jnp.bfloat16),
            pltpu.VMEM(padded, jnp.bfloat16),
            pltpu.SemaphoreType.DMA((4,)),
            pltpu.SemaphoreType.DMA((2 * HALVES,)),
        ],
        compiler_params=pltpu.CompilerParams(vmem_limit_bytes=60 * 2**20),
        name="pack_rows",
    )(owners, text_only, queries, grad_out)


def unpack_kernel(slot_ref, first_ref, second_ref, out_hbm, rows_ref, sems):
    rows = rows_ref.shape[0]
    parts = sems.shape[0]
    share = rows // parts
    copies = []
    for part in range(parts):
        @pl.loop(0, share // 8)
        def _(group, part=part):
            for inner in range(8):
                row = part * share + group * 8 + inner
                slot = slot_ref[row]
                for half, slots_ref in enumerate((first_ref, second_ref)):
                    slab = slots_ref[jnp.maximum(slot, 0)]
                    rows_ref[row, half * DEPTH:(half + 1) * DEPTH] = jnp.where(
                        slot >= 0, slab, jnp.zeros_like(slab)
                    )

        piece = pl.ds(part * share, share)
        copy = pltpu.make_async_copy(rows_ref.at[piece], out_hbm.at[piece], sems.at[part])
        copy.start()
        copies.append(copy)
    for copy in copies:
        copy.wait()


def unpack(slot_of, first, second):
    rows = (slot_of.shape[0], HALVES * DEPTH, HEAD)
    vmem = pl.BlockSpec(memory_space=pltpu.VMEM)
    return pl.pallas_call(
        unpack_kernel,
        out_shape=jax.ShapeDtypeStruct(rows, jnp.bfloat16),
        in_specs=[pl.BlockSpec(memory_space=pltpu.SMEM), vmem, vmem],
        out_specs=pl.BlockSpec(memory_space=pltpu.HBM),
        scratch_shapes=[pltpu.VMEM(rows, jnp.bfloat16), pltpu.SemaphoreType.DMA((4,))],
        compiler_params=pltpu.CompilerParams(vmem_limit_bytes=16 * 2**20),
        name="unpack_rows",
    )(slot_of, first, second)


def nt_dot(a, b):
    return lax.dot_general(a, b, (((1,), (1,)), ((), ())), preferred_element_type=jnp.float32)


def nn_dot(a, b):
    return jnp.dot(a, b, preferred_element_type=jnp.float32)


def softmax_terms(key_value_ref, live, query, grad, gate):
    keys = key_value_ref.shape[0] // 2
    cols = query.shape[0]
    scores = nt_dot(key_value_ref[:live], query)
    grad_probs = nt_dot(key_value_ref[keys:keys + live], grad)
    tops, expos, grads, sums, dots = [], [], [], [], []
    for start in range(0, live, CHUNK):
        score = scores[start:start + CHUNK].reshape(CHUNK // 8, 8, cols)
        top = jnp.max(score, axis=0)
        expo = jnp.exp2((score - top) * (SCALE * math.log2(math.e)))
        grad_prob = grad_probs[start:start + CHUNK].reshape(CHUNK // 8, 8, cols)
        tops.append(top)
        expos.append(expo)
        grads.append(grad_prob)
        sums.append(jnp.sum(expo, axis=0))
        dots.append(jnp.sum(expo * grad_prob, axis=0))
    largest = tops[0]
    for top in tops[1:]:
        largest = jnp.maximum(largest, top)
    largest = jnp.max(largest, axis=0, keepdims=True)
    factors = [jnp.exp2((top - largest) * (SCALE * math.log2(math.e))) for top in tops]
    total = sum(factor * part for factor, part in zip(factors, sums))
    delta = sum(factor * part for factor, part in zip(factors, dots))
    inverse = 1.0 / jnp.sum(total, axis=0, keepdims=True)
    delta = jnp.sum(delta, axis=0, keepdims=True) * inverse
    factors = [factor * (inverse * gate) for factor in factors]
    return expos, grads, factors, jnp.broadcast_to(delta, (8, cols))


def find_slots(received, place_list, slot_list):
    peers = received.shape[0] // (2 * CAP)
    found = jnp.int32(0)
    spare = jnp.int32(0)
    for peer in range(peers):
        used = jnp.zeros((16, HEAD), jnp.float32)
        for rank in range(CAP):
            first = received[peer * 2 * CAP + CAP + rank, 0:16].astype(jnp.float32)
            used = used + jnp.where(first < jnp.inf, 1.0, 0.0)
            place_list[found + rank] = jnp.int32(peer * 2 * CAP + rank)
            slot_list[found + rank] = jnp.int32(peer * CAP + rank)
        count = used[0, 0].astype(jnp.int32)
        spare = jnp.where(count < CAP, jnp.int32(peer), spare)
        found = found + count
    for extra in range(GROUP):
        place_list[found + extra] = spare * (2 * CAP) + (CAP - 1)
        slot_list[found + extra] = spare * CAP + (CAP - 1)
    return found


def gather_block(block, found, place_list, received, query_cols, grad_cols, start):
    for lane in range(GROUP):
        index = block * GROUP + lane
        place = place_list[index]
        grad = received[place + CAP]
        at = start + lane * DEPTH
        query_cols[at:at + DEPTH] = received[place]
        grad_cols[at:at + DEPTH] = jnp.where(index < found, grad, jnp.zeros_like(grad))


def query_grad_kernel(
    tiles_ref, gate_ref, key_value_ref, turned_ref, received, out_ref,
    place_list, slot_list, query_cols, grad_cols, score_grads,
):
    found = find_slots(received, place_list, slot_list)

    def work(live):
        @pl.loop(0, (found + (GROUP - 1)) // GROUP)
        def _(block):
            gather_block(block, found, place_list, received, query_cols, grad_cols, 0)
            for start in range(0, GROUP * DEPTH, SUB):
                expos, grads, factors, delta = softmax_terms(
                    key_value_ref, live,
                    query_cols[start:start + SUB], grad_cols[start:start + SUB], gate_ref[...],
                )
                for number, (expo, grad, factor) in enumerate(zip(expos, grads, factors)):
                    score_grad = expo * factor * (grad - delta)
                    score_grads[number * CHUNK:(number + 1) * CHUNK, start:start + SUB] = (
                        score_grad.reshape(CHUNK, SUB).astype(jnp.bfloat16)
                    )
                turned = nn_dot(turned_ref[:, :live], score_grads[:live, start:start + SUB])
                slabs = (turned * SCALE).T.astype(jnp.bfloat16).reshape(SUB // DEPTH, DEPTH, HEAD)
                for lane in range(SUB // DEPTH):
                    out_ref[slot_list[block * GROUP + start // DEPTH + lane]] = slabs[lane]

    most = key_value_ref.shape[0] // 2 // TILE
    for count in range(1, most + 1):
        @pl.when(tiles_ref[0] == count)
        def _(count=count):
            work(count * TILE)


def query_grads(tile_counts, gate, key_values, key_turned, received):
    slots = received.shape[0] // 2
    keys = key_values.shape[0] // 2
    cols = GROUP * DEPTH
    smem = pl.BlockSpec(memory_space=pltpu.SMEM)
    vmem = pl.BlockSpec(memory_space=pltpu.VMEM)
    return pl.pallas_call(
        query_grad_kernel,
        out_shape=jax.ShapeDtypeStruct((slots, DEPTH, HEAD), jnp.bfloat16),
        in_specs=[smem, vmem, vmem, vmem, vmem],
        out_specs=vmem,
        scratch_shapes=[
            pltpu.SMEM((slots + GROUP,), jnp.int32),
            pltpu.SMEM((slots + GROUP,), jnp.int32),
            pltpu.VMEM((cols, HEAD), jnp.bfloat16),
            pltpu.VMEM((cols, HEAD), jnp.bfloat16),
            pltpu.VMEM((keys, cols), jnp.bfloat16),
        ],
        compiler_params=pltpu.CompilerParams(vmem_limit_bytes=32 * 2**20),
        name="query_grads",
    )(tile_counts, gate, key_values, key_turned, received)


def image_grad_kernel(
    tiles_ref, gate_ref, key_value_ref, first_ref, second_ref, after_first, after_second,
    grad_key_ref, grad_value_ref,
    place_list, slot_list, key_sum, value_sum, query_cols, grad_cols, score_grads, weights,
):
    del after_first, after_second
    found = find_slots(first_ref, place_list, slot_list)
    key_sum[...] = jnp.zeros(key_sum.shape, jnp.float32)
    value_sum[...] = jnp.zeros(value_sum.shape, jnp.float32)

    def work(live):
        @pl.loop(0, (found + (GROUP - 1)) // GROUP)
        def _(block):
            for half, received in enumerate((first_ref, second_ref)):
                start = half * GROUP * DEPTH
                gather_block(block, found, place_list, received, query_cols, grad_cols, start)
                expos, grads, factors, delta = softmax_terms(
                    key_value_ref, live,
                    query_cols[start:start + SUB], grad_cols[start:start + SUB],
                    gate_ref[half:half + 1],
                )
                for number, (expo, grad, factor) in enumerate(zip(expos, grads, factors)):
                    rows = slice(number * CHUNK, (number + 1) * CHUNK)
                    weighted = expo * factor
                    score_grad = weighted * (grad - delta)
                    weights[rows, start:start + SUB] = (
                        weighted.reshape(CHUNK, SUB).astype(jnp.bfloat16)
                    )
                    score_grads[rows, start:start + SUB] = (
                        score_grad.reshape(CHUNK, SUB).astype(jnp.bfloat16)
                    )
            key_sum[:live] += nn_dot(score_grads[:live], query_cols[...])
            value_sum[:live] += nn_dot(weights[:live], grad_cols[...])

    most = key_value_ref.shape[0] // 2 // TILE
    for count in range(1, most + 1):
        @pl.when(tiles_ref[0] == count)
        def _(count=count):
            work(count * TILE)

    grad_key_ref[...] = (key_sum[...] * SCALE).astype(jnp.bfloat16)
    grad_value_ref[...] = value_sum[...].astype(jnp.bfloat16)


def image_grads(tile_counts, gate, key_values, first, second, after):
    slots = first.shape[0] // 2
    keys = key_values.shape[0] // 2
    cols = HALVES * GROUP * DEPTH
    smem = pl.BlockSpec(memory_space=pltpu.SMEM)
    vmem = pl.BlockSpec(memory_space=pltpu.VMEM)
    return pl.pallas_call(
        image_grad_kernel,
        out_shape=(
            jax.ShapeDtypeStruct((keys, HEAD), jnp.bfloat16),
            jax.ShapeDtypeStruct((keys, HEAD), jnp.bfloat16),
        ),
        in_specs=[smem, vmem, vmem, vmem, vmem] + [pl.BlockSpec(memory_space=pl.ANY)] * HALVES,
        out_specs=(vmem, vmem),
        scratch_shapes=[
            pltpu.SMEM((slots + GROUP,), jnp.int32),
            pltpu.SMEM((slots + GROUP,), jnp.int32),
            pltpu.VMEM((keys, HEAD), jnp.float32),
            pltpu.VMEM((keys, HEAD), jnp.float32),
            pltpu.VMEM((cols, HEAD), jnp.bfloat16),
            pltpu.VMEM((cols, HEAD), jnp.bfloat16),
            pltpu.VMEM((keys, cols), jnp.bfloat16),
            pltpu.VMEM((keys, cols), jnp.bfloat16),
        ],
        compiler_params=pltpu.CompilerParams(vmem_limit_bytes=32 * 2**20),
        cost_estimate=pl.CostEstimate(
            flops=8 * first.shape[0] * 16 * keys * HEAD,
            bytes_accessed=4 * 2**20,
            transcendentals=first.shape[0] * 16 * keys,
        ),
        name="image_grads",
    )(tile_counts, gate, key_values, first, second, *after)


def on_device(
    queries, grad_out, image_keys, image_values, gate_logits, tile_counts, owners, text_only
):
    rows, tokens, width = queries.shape
    heads = width // HEAD
    peers = lax.axis_size("dp")

    def slabs(array):
        split = array.reshape(rows, tokens, heads, HEAD).transpose(0, 2, 1, 3)
        return split.reshape(rows, heads * tokens, HEAD)

    *sends, slot_of = pack(owners[:, 0], text_only, slabs(queries), slabs(grad_out), peers)

    def exchange(array):
        return lax.all_to_all(array, "dp", split_axis=0, concat_axis=0, tiled=True)

    received = [exchange(send).reshape(peers * 2 * CAP, DEPTH, HEAD) for send in sends]
    key_values = jnp.concatenate([image_keys[0], image_values[0]])
    key_turned = image_keys[0].T
    gate = jnp.repeat(jnp.tanh(gate_logits), tokens).reshape(HALVES, DEPTH)
    gate = jnp.tile(gate, (1, SUB // DEPTH))
    grad_slots = [
        query_grads(tile_counts, gate[half:half + 1], key_values, key_turned, received[half])
        for half in range(HALVES)
    ]
    returned = [
        exchange(grads.reshape(peers, CAP, DEPTH, HEAD)).reshape(peers * CAP, DEPTH, HEAD)
        for grads in grad_slots
    ]
    grad_key, grad_value = image_grads(
        tile_counts, gate, key_values, received[0], received[1], grad_slots
    )
    grad_rows = unpack(slot_of, returned[0], returned[1])
    grad_rows = grad_rows.reshape(rows, heads, tokens, HEAD).transpose(0, 2, 1, 3)
    return grad_rows.reshape(rows, tokens, width), grad_key[None], grad_value[None]


def solution(mesh):
    placed = (
        P("dp", None, "tensor"),
        P("dp", None, "tensor"),
        P("dp", None, "tensor"),
        P("dp", None, "tensor"),
        P("tensor"),
        P("dp"),
        P("dp", None),
        P("dp"),
    )
    return jax.shard_map(
        on_device,
        mesh=mesh,
        in_specs=placed,
        out_specs=(P("dp", None, "tensor"), P("dp", None, "tensor"), P("dp", None, "tensor")),
        check_vma=False,
    )
```

```python
import math

import jax
import jax.numpy as jnp
from jax import lax
from jax.experimental import pallas as pl
from jax.experimental.pallas import tpu as pltpu
from jax.sharding import PartitionSpec as P

HEAD = 128
TILE = 256
CAP = 3
SUB = 256
GROUP = 16
DEPTH = 16
HALVES = 2
CHUNK = 128
SCALE = HEAD ** (-0.5)


def pack_kernel(
    owner_hbm, text_hbm, query_hbm, grad_hbm, send_first, send_second, slot_ref,
    owners, texts, count, place_of, query_rows, grad_rows, query_slots, grad_slots,
    in_sems, out_sems,
):
    rows = query_rows.shape[0]
    peers = query_slots.shape[0] - 1
    send_refs = (send_first, send_second)
    owner_copy = pltpu.make_async_copy(owner_hbm, owners, in_sems.at[0])
    text_copy = pltpu.make_async_copy(text_hbm, texts, in_sems.at[1])
    query_copy = pltpu.make_async_copy(query_hbm, query_rows, in_sems.at[2])
    grad_copy = pltpu.make_async_copy(grad_hbm, grad_rows, in_sems.at[3])
    owner_copy.start()
    text_copy.start()
    query_copy.start()
    grad_copy.start()
    for peer in range(peers):
        count[peer] = 0
    query_slots[...] = jnp.zeros(query_slots.shape, query_slots.dtype)
    grad_slots[...] = jnp.full(grad_slots.shape, jnp.inf, grad_slots.dtype)
    owner_copy.wait()
    text_copy.wait()

    @pl.loop(0, rows // 8)
    def _(group):
        for inner in range(8):
            row = group * 8 + inner
            owner = owners[row]
            live = texts[row] == 0
            rank = count[owner]
            count[owner] = rank + jnp.where(live, 1, 0)
            place_of[row] = jnp.where(live, owner * 4 + rank, peers * 4)
            slot_ref[row] = jnp.where(live, owner * CAP + rank, -1)

    out_copies = []
    for which, (copy, source, target) in enumerate(
        ((query_copy, query_rows, query_slots), (grad_copy, grad_rows, grad_slots))
    ):
        copy.wait()

        @pl.loop(0, rows // 8)
        def _(group, source=source, target=target):
            for inner in range(8):
                row = group * 8 + inner
                place = place_of[row]
                target[place >> 2, place & 3] = source[row]

        for half, send in enumerate(send_refs):
            out = pltpu.make_async_copy(
                target.at[pl.ds(0, peers), :, pl.ds(half * DEPTH, DEPTH)],
                send.at[:, pl.ds(which * CAP, CAP)],
                out_sems.at[which * HALVES + half],
            )
            out.start()
            out_copies.append(out)
    for out in out_copies:
        out.wait()


def pack(owners, text_only, queries, grad_out, peers):
    rows = queries.shape[0]
    slab = queries.shape[1:]
    hbm = pl.BlockSpec(memory_space=pltpu.HBM)
    padded = (peers + 1, CAP) + slab
    return pl.pallas_call(
        pack_kernel,
        out_shape=(
            jax.ShapeDtypeStruct((peers, 2 * CAP, DEPTH, HEAD), jnp.bfloat16),
            jax.ShapeDtypeStruct((peers, 2 * CAP, DEPTH, HEAD), jnp.bfloat16),
            jax.ShapeDtypeStruct((rows,), jnp.int32),
        ),
        in_specs=[hbm, hbm, hbm, hbm],
        out_specs=(hbm, hbm, pl.BlockSpec(memory_space=pltpu.SMEM)),
        scratch_shapes=[
            pltpu.SMEM((rows,), jnp.int32),
            pltpu.SMEM((rows,), jnp.int32),
            pltpu.SMEM((peers,), jnp.int32),
            pltpu.SMEM((rows,), jnp.int32),
            pltpu.VMEM((rows,) + slab, jnp.bfloat16),
            pltpu.VMEM((rows,) + slab, jnp.bfloat16),
            pltpu.VMEM(padded, jnp.bfloat16),
            pltpu.VMEM(padded, jnp.bfloat16),
            pltpu.SemaphoreType.DMA((4,)),
            pltpu.SemaphoreType.DMA((2 * HALVES,)),
        ],
        compiler_params=pltpu.CompilerParams(vmem_limit_bytes=60 * 2**20),
        name="pack_rows",
    )(owners, text_only, queries, grad_out)


def unpack_kernel(slot_ref, first_ref, second_ref, out_hbm, rows_ref, sems):
    rows = rows_ref.shape[0]
    parts = sems.shape[0]
    share = rows // parts
    copies = []
    for part in range(parts):
        @pl.loop(0, share // 8)
        def _(group, part=part):
            for inner in range(8):
                row = part * share + group * 8 + inner
                slot = slot_ref[row]
                for half, slots_ref in enumerate((first_ref, second_ref)):
                    slab = slots_ref[jnp.maximum(slot, 0)]
                    rows_ref[row, half * DEPTH:(half + 1) * DEPTH] = jnp.where(
                        slot >= 0, slab, jnp.zeros_like(slab)
                    )

        piece = pl.ds(part * share, share)
        copy = pltpu.make_async_copy(rows_ref.at[piece], out_hbm.at[piece], sems.at[part])
        copy.start()
        copies.append(copy)
    for copy in copies:
        copy.wait()


def unpack(slot_of, first, second):
    rows = (slot_of.shape[0], HALVES * DEPTH, HEAD)
    vmem = pl.BlockSpec(memory_space=pltpu.VMEM)
    return pl.pallas_call(
        unpack_kernel,
        out_shape=jax.ShapeDtypeStruct(rows, jnp.bfloat16),
        in_specs=[pl.BlockSpec(memory_space=pltpu.SMEM), vmem, vmem],
        out_specs=pl.BlockSpec(memory_space=pltpu.HBM),
        scratch_shapes=[pltpu.VMEM(rows, jnp.bfloat16), pltpu.SemaphoreType.DMA((4,))],
        compiler_params=pltpu.CompilerParams(vmem_limit_bytes=16 * 2**20),
        name="unpack_rows",
    )(slot_of, first, second)


def nt_dot(a, b):
    return lax.dot_general(a, b, (((1,), (1,)), ((), ())), preferred_element_type=jnp.float32)


def nn_dot(a, b):
    return jnp.dot(a, b, preferred_element_type=jnp.float32)


def softmax_terms(key_value_ref, live, query, grad, gate):
    keys = key_value_ref.shape[0] // 2
    cols = query.shape[0]
    scores = nt_dot(key_value_ref[:live], query)
    grad_probs = nt_dot(key_value_ref[keys:keys + live], grad)
    tops, expos, grads, sums, dots = [], [], [], [], []
    for start in range(0, live, CHUNK):
        score = scores[start:start + CHUNK].reshape(CHUNK // 8, 8, cols)
        top = jnp.max(score, axis=0)
        expo = jnp.exp2((score - top) * (SCALE * math.log2(math.e)))
        grad_prob = grad_probs[start:start + CHUNK].reshape(CHUNK // 8, 8, cols)
        tops.append(top)
        expos.append(expo)
        grads.append(grad_prob)
        sums.append(jnp.sum(expo, axis=0))
        dots.append(jnp.sum(expo * grad_prob, axis=0))
    largest = tops[0]
    for top in tops[1:]:
        largest = jnp.maximum(largest, top)
    largest = jnp.max(largest, axis=0, keepdims=True)
    factors = [jnp.exp2((top - largest) * (SCALE * math.log2(math.e))) for top in tops]
    total = sum(factor * part for factor, part in zip(factors, sums))
    delta = sum(factor * part for factor, part in zip(factors, dots))
    inverse = 1.0 / jnp.sum(total, axis=0, keepdims=True)
    delta = jnp.sum(delta, axis=0, keepdims=True) * inverse
    factors = [factor * (inverse * gate) for factor in factors]
    return expos, grads, factors, jnp.broadcast_to(delta, (8, cols))


def find_slots(received, place_list, slot_list):
    peers = received.shape[0] // (2 * CAP)
    found = jnp.int32(0)
    spare = jnp.int32(0)
    for peer in range(peers):
        used = jnp.zeros((16, HEAD), jnp.float32)
        for rank in range(CAP):
            first = received[peer * 2 * CAP + CAP + rank, 0:16].astype(jnp.float32)
            used = used + jnp.where(first < jnp.inf, 1.0, 0.0)
            place_list[found + rank] = jnp.int32(peer * 2 * CAP + rank)
            slot_list[found + rank] = jnp.int32(peer * CAP + rank)
        count = used[0, 0].astype(jnp.int32)
        spare = jnp.where(count < CAP, jnp.int32(peer), spare)
        found = found + count
    for extra in range(GROUP):
        place_list[found + extra] = spare * (2 * CAP) + (CAP - 1)
        slot_list[found + extra] = spare * CAP + (CAP - 1)
    return found


def gather_block(block, found, place_list, received, query_cols, grad_cols, start):
    for lane in range(GROUP):
        index = block * GROUP + lane
        place = place_list[index]
        grad = received[place + CAP]
        at = start + lane * DEPTH
        query_cols[at:at + DEPTH] = received[place]
        grad_cols[at:at + DEPTH] = jnp.where(index < found, grad, jnp.zeros_like(grad))


def query_grad_kernel(
    tiles_ref, gate_ref, key_value_ref, turned_ref, received, out_ref,
    place_list, slot_list, query_cols, grad_cols, score_grads,
):
    found = find_slots(received, place_list, slot_list)

    def work(live):
        @pl.loop(0, (found + (GROUP - 1)) // GROUP)
        def _(block):
            gather_block(block, found, place_list, received, query_cols, grad_cols, 0)
            for start in range(0, GROUP * DEPTH, SUB):
                expos, grads, factors, delta = softmax_terms(
                    key_value_ref, live,
                    query_cols[start:start + SUB], grad_cols[start:start + SUB], gate_ref[...],
                )
                for number, (expo, grad, factor) in enumerate(zip(expos, grads, factors)):
                    score_grad = expo * factor * (grad - delta)
                    score_grads[number * CHUNK:(number + 1) * CHUNK, start:start + SUB] = (
                        score_grad.reshape(CHUNK, SUB).astype(jnp.bfloat16)
                    )
                turned = nn_dot(turned_ref[:, :live], score_grads[:live, start:start + SUB])
                slabs = (turned * SCALE).T.astype(jnp.bfloat16).reshape(SUB // DEPTH, DEPTH, HEAD)
                for lane in range(SUB // DEPTH):
                    out_ref[slot_list[block * GROUP + start // DEPTH + lane]] = slabs[lane]

    most = key_value_ref.shape[0] // 2 // TILE
    for count in range(1, most + 1):
        @pl.when(tiles_ref[0] == count)
        def _(count=count):
            work(count * TILE)


def query_grads(tile_counts, gate, key_values, key_turned, received):
    slots = received.shape[0] // 2
    keys = key_values.shape[0] // 2
    cols = GROUP * DEPTH
    smem = pl.BlockSpec(memory_space=pltpu.SMEM)
    vmem = pl.BlockSpec(memory_space=pltpu.VMEM)
    return pl.pallas_call(
        query_grad_kernel,
        out_shape=jax.ShapeDtypeStruct((slots, DEPTH, HEAD), jnp.bfloat16),
        in_specs=[smem, vmem, vmem, vmem, vmem],
        out_specs=vmem,
        scratch_shapes=[
            pltpu.SMEM((slots + GROUP,), jnp.int32),
            pltpu.SMEM((slots + GROUP,), jnp.int32),
            pltpu.VMEM((cols, HEAD), jnp.bfloat16),
            pltpu.VMEM((cols, HEAD), jnp.bfloat16),
            pltpu.VMEM((keys, cols), jnp.bfloat16),
        ],
        compiler_params=pltpu.CompilerParams(vmem_limit_bytes=32 * 2**20),
        name="query_grads",
    )(tile_counts, gate, key_values, key_turned, received)


def image_grad_kernel(
    tiles_ref, gate_ref, key_value_ref, first_ref, second_ref, after_first, after_second,
    grad_key_ref, grad_value_ref,
    place_list, slot_list, key_sum, value_sum, query_cols, grad_cols, score_grads, weights,
):
    del after_first, after_second
    found = find_slots(first_ref, place_list, slot_list)
    key_sum[...] = jnp.zeros(key_sum.shape, jnp.float32)
    value_sum[...] = jnp.zeros(value_sum.shape, jnp.float32)

    def work(live):
        @pl.loop(0, (found + (GROUP - 1)) // GROUP)
        def _(block):
            for half, received in enumerate((first_ref, second_ref)):
                start = half * GROUP * DEPTH
                gather_block(block, found, place_list, received, query_cols, grad_cols, start)
                expos, grads, factors, delta = softmax_terms(
                    key_value_ref, live,
                    query_cols[start:start + SUB], grad_cols[start:start + SUB],
                    gate_ref[half:half + 1],
                )
                for number, (expo, grad, factor) in enumerate(zip(expos, grads, factors)):
                    rows = slice(number * CHUNK, (number + 1) * CHUNK)
                    weighted = expo * factor
                    score_grad = weighted * (grad - delta)
                    weights[rows, start:start + SUB] = (
                        weighted.reshape(CHUNK, SUB).astype(jnp.bfloat16)
                    )
                    score_grads[rows, start:start + SUB] = (
                        score_grad.reshape(CHUNK, SUB).astype(jnp.bfloat16)
                    )
            key_sum[:live] += nn_dot(score_grads[:live], query_cols[...])
            value_sum[:live] += nn_dot(weights[:live], grad_cols[...])

    most = key_value_ref.shape[0] // 2 // TILE
    for count in range(1, most + 1):
        @pl.when(tiles_ref[0] == count)
        def _(count=count):
            work(count * TILE)

    grad_key_ref[...] = (key_sum[...] * SCALE).astype(jnp.bfloat16)
    grad_value_ref[...] = value_sum[...].astype(jnp.bfloat16)


def image_grads(tile_counts, gate, key_values, first, second, after):
    slots = first.shape[0] // 2
    keys = key_values.shape[0] // 2
    cols = HALVES * GROUP * DEPTH
    smem = pl.BlockSpec(memory_space=pltpu.SMEM)
    vmem = pl.BlockSpec(memory_space=pltpu.VMEM)
    return pl.pallas_call(
        image_grad_kernel,
        out_shape=(
            jax.ShapeDtypeStruct((keys, HEAD), jnp.bfloat16),
            jax.ShapeDtypeStruct((keys, HEAD), jnp.bfloat16),
        ),
        in_specs=[smem, vmem, vmem, vmem, vmem] + [pl.BlockSpec(memory_space=pl.ANY)] * HALVES,
        out_specs=(vmem, vmem),
        scratch_shapes=[
            pltpu.SMEM((slots + GROUP,), jnp.int32),
            pltpu.SMEM((slots + GROUP,), jnp.int32),
            pltpu.VMEM((keys, HEAD), jnp.float32),
            pltpu.VMEM((keys, HEAD), jnp.float32),
            pltpu.VMEM((cols, HEAD), jnp.bfloat16),
            pltpu.VMEM((cols, HEAD), jnp.bfloat16),
            pltpu.VMEM((keys, cols), jnp.bfloat16),
            pltpu.VMEM((keys, cols), jnp.bfloat16),
        ],
        compiler_params=pltpu.CompilerParams(vmem_limit_bytes=32 * 2**20),
        cost_estimate=pl.CostEstimate(
            flops=8 * first.shape[0] * 16 * keys * HEAD,
            bytes_accessed=4 * 2**20,
            transcendentals=first.shape[0] * 16 * keys,
        ),
        name="image_grads",
    )(tile_counts, gate, key_values, first, second, *after)


def prepare_kernel(key_ref, value_ref, send_in, send_out, key_value_ref, turned_ref):
    del send_in, send_out
    keys = key_ref.shape[0]
    key_value_ref[:keys] = key_ref[...]
    key_value_ref[keys:] = value_ref[...]
    turned_ref[...] = key_ref[...].T


def prepare(key_rows, value_rows, send):
    keys = key_rows.shape[0]
    vmem = pl.BlockSpec(memory_space=pltpu.VMEM)
    hbm = pl.BlockSpec(memory_space=pltpu.HBM)
    return pl.pallas_call(
        prepare_kernel,
        out_shape=(
            jax.ShapeDtypeStruct(send.shape, send.dtype),
            jax.ShapeDtypeStruct((2 * keys, HEAD), jnp.bfloat16),
            jax.ShapeDtypeStruct((HEAD, keys), jnp.bfloat16),
        ),
        in_specs=[vmem, vmem, hbm],
        out_specs=(hbm, vmem, vmem),
        input_output_aliases={2: 0},
        compiler_params=pltpu.CompilerParams(vmem_limit_bytes=60 * 2**20),
        cost_estimate=pl.CostEstimate(
            flops=0, bytes_accessed=6 * 2 * keys * HEAD, transcendentals=0
        ),
        name="prepare_keys",
    )(key_rows, value_rows, send)


def on_device(
    queries, grad_out, image_keys, image_values, gate_logits, tile_counts, owners, text_only
):
    rows, tokens, width = queries.shape
    heads = width // HEAD
    peers = lax.axis_size("dp")

    def slabs(array):
        split = array.reshape(rows, tokens, heads, HEAD).transpose(0, 2, 1, 3)
        return split.reshape(rows, heads * tokens, HEAD)

    *sends, slot_of = pack(owners[:, 0], text_only, slabs(queries), slabs(grad_out), peers)

    def exchange(array):
        return lax.all_to_all(array, "dp", split_axis=0, concat_axis=0, tiled=True)

    sends[1], key_values, key_turned = prepare(image_keys[0], image_values[0], sends[1])
    received = [exchange(send).reshape(peers * 2 * CAP, DEPTH, HEAD) for send in sends]
    gate = jnp.repeat(jnp.tanh(gate_logits), tokens).reshape(HALVES, DEPTH)
    gate = jnp.tile(gate, (1, SUB // DEPTH))
    grad_slots = [
        query_grads(tile_counts, gate[half:half + 1], key_values, key_turned, received[half])
        for half in range(HALVES)
    ]
    returned = [
        exchange(grads.reshape(peers, CAP, DEPTH, HEAD)).reshape(peers * CAP, DEPTH, HEAD)
        for grads in grad_slots
    ]
    grad_key, grad_value = image_grads(
        tile_counts, gate, key_values, received[0], received[1], grad_slots
    )
    grad_rows = unpack(slot_of, returned[0], returned[1])
    grad_rows = grad_rows.reshape(rows, heads, tokens, HEAD).transpose(0, 2, 1, 3)
    return grad_rows.reshape(rows, tokens, width), grad_key[None], grad_value[None]


def solution(mesh):
    placed = (
        P("dp", None, "tensor"),
        P("dp", None, "tensor"),
        P("dp", None, "tensor"),
        P("dp", None, "tensor"),
        P("tensor"),
        P("dp"),
        P("dp", None),
        P("dp"),
    )
    return jax.shard_map(
        on_device,
        mesh=mesh,
        in_specs=placed,
        out_specs=(P("dp", None, "tensor"), P("dp", None, "tensor"), P("dp", None, "tensor")),
        check_vma=False,
    )
```
